32 devices in a mesh: grp: 2 (over x), bl: 16 (over z, y, core).
Axes of the slice: x: 2, y: 2, z: 4, core: 2. Of those that a mesh axis runs over, the one named last changes fastest.
Arguments:
- station_gains: float32 [16, 8, 40, 512], P('grp', None, None, 'bl'), parts along dimension 0, may hold values from -3 to 3
- model_visibilities: bfloat16 [16, 8, 8, 40, 2048], P('grp', None, None, None, 'bl'), parts along dimension 0, may hold values from -0.65625 to 0.65625
- observed: float32 [16, 8, 8, 2048], P('grp', None, None, 'bl'), parts along dimension 0, may hold values from -6 to 6
- weights: float32 [16, 8, 2048], P('grp', None, 'bl'), parts along dimension 0, may hold values from 0.005 to 0.05
- kept_visibility_mask: int32 [16, 8, 2048], P('grp', None, 'bl'), parts along dimension 0, may hold values 0 or 1
- first_station: int32 [2048], P('bl'), may hold values from 0 to 511, as said below
- second_station: int32 [2048], P('bl'), may hold values from 0 to 511, as said below
Outputs:
- gradient: float32 [16, 8, 40, 512], P('grp', None, None, 'bl'), parts along dimension 0
The draws below stay inside these ranges and needn't reach their ends.
There are 2 independent parts, one for each index of `grp`. The reference program is written for one: setup_inputs(seed, part) draws one part's arguments, and reference() takes and returns one part's arrays. A program takes and returns all parts, laid end to end along the dimension named above; an argument that names none is the same for every part. Nothing has to cross between parts.
Inputs may be any that keep to these rules, and one draw needn't show every extreme that they name: Baselines come in blocks of 128; in block k, with h = k // 8 and l = k % 8, every first_station lies in [h * 8 * 32, (h + 1) * 8 * 32), every second_station s has (s // 32) % 8 == l, the two stations of a baseline differ, and no pair repeats within a block. `second_station`: see first_station.
All inputs are finite; a program needn't handle non-finite values. No bound on the sum of `kept_visibility_mask` on one device may be relied on, other than what follows from the above.
Results may differ from the reference program's by a relative error of at most 0.0003.
Values sent between devices are 32-bit elements; how exact they have to be, the bound alone decides.
A program may use at most 64 MiB of HBM per device.

```python
import math
import jax
import jax.numpy as jnp
from jax import lax

STATIONS = 512
DIRECTION_COUNT = 40
CHANNEL_COUNT = 8
TIMESLOT_COUNT = 8
GROUP = 8
BASELINE_SHARE = 128
BASELINE_TOTAL = 2048
N_BL = 16


def baseline_pairs(key):
    per_device = STATIONS // N_BL
    row_span = GROUP * per_device
    col_span = N_BL // GROUP * per_device
    pair_count = row_span * col_span

    def one_block(block_key, device_at):
        upper_group = device_at // GROUP
        lower_group = device_at % GROUP
        shuffled = jax.random.permutation(block_key, pair_count).astype(jnp.int32)
        row_pos = shuffled // col_span
        col_pos = shuffled % col_span
        leading = upper_group * row_span + row_pos
        trailing = (col_pos // per_device * GROUP + lower_group) * per_device + col_pos % per_device
        clash = (leading == trailing).astype(jnp.int32)
        ranked = jnp.argsort(jnp.arange(pair_count, dtype=jnp.int32) + pair_count * clash)
        chosen = ranked[:BASELINE_SHARE]
        return (leading[chosen], trailing[chosen])
    block_keys = jax.random.split(key, N_BL)
    leading, trailing = jax.vmap(one_block)(block_keys, jnp.arange(N_BL, dtype=jnp.int32))
    return (leading.reshape(-1).astype(jnp.int32), trailing.reshape(-1).astype(jnp.int32))


def draw_first_station(key, part):
    leading, trailing = baseline_pairs(key)
    return leading


def draw_second_station(key, part):
    leading, trailing = baseline_pairs(key)
    return trailing


def touch_ends(values, stream_key, smallest, largest):
    spot = [jax.random.randint(jax.random.fold_in(stream_key, axis), (), 0, length) for axis, length in enumerate(values.shape)]
    widest = values.shape.index(max(values.shape))
    beside = spot[:widest] + [(spot[widest] + 1) % values.shape[widest]] + spot[widest + 1:]
    return values.at[tuple(spot)].set(smallest).at[tuple(beside)].set(largest)


def levels(stream_key, extent, cuts, smallest, largest):
    loudness = 1.0
    for axis_at, blocks in cuts:
        draws = jax.random.uniform(jax.random.fold_in(jax.random.fold_in(stream_key, 6), axis_at), (blocks,), jnp.float32, smallest / len(cuts), largest / len(cuts))
        loudness = loudness * jnp.repeat(jnp.exp(draws), extent[axis_at] // blocks).reshape((-1,) + (1,) * (len(extent) - 1 - axis_at))
    return loudness


def noise(key, dims, width, most, shards=(), kind=jnp.bfloat16):
    gain = levels(key, dims, shards, -0.22, 0.18) if shards else 1.0
    values = jax.random.normal(key, dims, jnp.float32) * width * gain
    return jnp.minimum(jnp.maximum(values, -most), most).astype(kind)


def setup_inputs(seed: int = 0, part: int = 0) -> dict:
    keys = jax.random.split(jax.random.key(seed), 8)
    part_splits = jax.random.split(jax.random.fold_in(keys[7], part), 8)
    station_gains = noise(part_splits[0], (CHANNEL_COUNT, 8, DIRECTION_COUNT, STATIONS), 0.5, 3.0, ((3, 16),), jnp.float32)
    model_visibilities = noise(part_splits[1], (CHANNEL_COUNT, TIMESLOT_COUNT, 8, DIRECTION_COUNT, BASELINE_TOTAL), 0.11, 0.65625, ((4, 16),))
    observed = noise(part_splits[2], (CHANNEL_COUNT, TIMESLOT_COUNT, 8, BASELINE_TOTAL), 1.0, 6.0, ((3, 16),), jnp.float32)
    weights = jnp.clip(jnp.exp(math.log(0.05) - 2.3025851 * jax.random.uniform(part_splits[3], (CHANNEL_COUNT, TIMESLOT_COUNT, BASELINE_TOTAL), jnp.float32) ** levels(part_splits[3], (CHANNEL_COUNT, TIMESLOT_COUNT, BASELINE_TOTAL), ((2, 16),), -0.2, 0.2)), 0.005, 0.05)
    kept_visibility_mask = touch_ends((jax.random.randint(part_splits[4], (CHANNEL_COUNT, TIMESLOT_COUNT, BASELINE_TOTAL), 0, 8) < 7).astype(jnp.int32), jax.random.fold_in(part_splits[4], 1), 0, 1)
    first_station = draw_first_station(jax.random.fold_in(keys[7], 71), part)
    second_station = draw_second_station(jax.random.fold_in(keys[7], 71), part)
    return {"station_gains": station_gains, "model_visibilities": model_visibilities, "observed": observed, "weights": weights, "kept_visibility_mask": kept_visibility_mask, "first_station": first_station, "second_station": second_station}


def unpack(array, axis):
    parts = [lax.index_in_dim(array, entry_at, axis, keepdims=False) for entry_at in range(8)]
    return (parts[:4], parts[4:])


def pack(jones, axis):
    return jnp.stack(jones[0] + jones[1], axis)


def jones_product(left_jones, right_jones):
    out_real = []
    out_imag = []
    for row_at in range(2):
        for col_at in range(2):
            total_real = 0.0
            total_imag = 0.0
            for middle in range(2):
                left_real = left_jones[0][2 * row_at + middle]
                left_imag = left_jones[1][2 * row_at + middle]
                right_real = right_jones[0][2 * middle + col_at]
                right_imag = right_jones[1][2 * middle + col_at]
                total_real = total_real + left_real * right_real - left_imag * right_imag
                total_imag = total_imag + left_real * right_imag + left_imag * right_real
            out_real.append(total_real)
            out_imag.append(total_imag)
    return (out_real, out_imag)


def hermitian(jones):
    order_list = [0, 2, 1, 3]
    return ([jones[0][entry_at] for entry_at in order_list], [-jones[1][entry_at] for entry_at in order_list])


def predict_block(lead_gain, trail_gain, model_block):
    left_jones = unpack(lead_gain[:, None], 2)
    right_jones = unpack(trail_gain[:, None], 2)
    sky_jones = unpack(model_block.astype(jnp.float32), 2)
    predicted = jones_product(jones_product(left_jones, sky_jones), hermitian(right_jones))
    summed = ([jnp.sum(part, axis=2) for part in predicted[0]], [jnp.sum(part, axis=2) for part in predicted[1]])
    return pack(summed, 2)


def gradient_block(lead_gain, trail_gain, model_block, weighted):
    left_jones = unpack(lead_gain[:, None], 2)
    right_jones = unpack(trail_gain[:, None], 2)
    sky_jones = unpack(model_block.astype(jnp.float32), 2)
    residual = unpack(weighted[:, :, :, None], 2)
    toward_lead = jones_product(residual, jones_product(right_jones, hermitian(sky_jones)))
    toward_trail = jones_product(hermitian(residual), jones_product(left_jones, sky_jones))
    lead_sum = ([jnp.sum(part, axis=1) for part in toward_lead[0]], [jnp.sum(part, axis=1) for part in toward_lead[1]])
    trail_sum = ([jnp.sum(part, axis=1) for part in toward_trail[0]], [jnp.sum(part, axis=1) for part in toward_trail[1]])
    return pack(lead_sum, 1), pack(trail_sum, 1)


def reference(station_gains, model_visibilities, observed, weights, kept_visibility_mask, first_station, second_station):
    count_of_blocks = BASELINE_TOTAL // BASELINE_SHARE
    live_weight = weights * kept_visibility_mask.astype(jnp.float32)

    def one_block(block_at, running):
        start_at = (block_at * BASELINE_SHARE).astype(jnp.int32)
        lead_ids = lax.dynamic_slice_in_dim(first_station, start_at, BASELINE_SHARE, 0)
        trail_ids = lax.dynamic_slice_in_dim(second_station, start_at, BASELINE_SHARE, 0)
        lead_gain = jnp.take(station_gains, lead_ids, axis=3)
        trail_gain = jnp.take(station_gains, trail_ids, axis=3)
        model_block = lax.dynamic_slice_in_dim(model_visibilities, start_at, BASELINE_SHARE, 4)
        observed_block = lax.dynamic_slice_in_dim(observed, start_at, BASELINE_SHARE, 3)
        live_block = lax.dynamic_slice_in_dim(live_weight, start_at, BASELINE_SHARE, 2)
        predicted = predict_block(lead_gain, trail_gain, model_block)
        weighted = (observed_block - predicted) * live_block[:, :, None, :]
        toward_lead, toward_trail = gradient_block(lead_gain, trail_gain, model_block, weighted)
        running = running.at[:, :, :, lead_ids].add(toward_lead)
        running = running.at[:, :, :, trail_ids].add(toward_trail)
        return running

    running = lax.fori_loop(0, count_of_blocks, one_block, jnp.zeros(station_gains.shape, jnp.float32))
    return -running
```

```python
import functools

import jax
import jax.numpy as jnp
from jax import lax
from jax.experimental import pallas as pl
from jax.experimental.pallas import tpu as pltpu
from jax.sharding import PartitionSpec as P

GROUP = 8
CHIPS = GROUP // 2
PAIR = 2
F32 = jnp.float32
BF16 = jnp.bfloat16


def split_dot(lhs, rhs, dims, split_left):
    wide = lhs if split_left else rhs
    high = wide.astype(BF16)
    low = (wide - high.astype(F32)).astype(BF16)
    total = None
    for half in (high, low):
        pair = (half, rhs) if split_left else (lhs, half)
        term = lax.dot_general(*pair, (dims, ((), ())), preferred_element_type=F32)
        total = term if total is None else total + term
    return total


def kernel(
    columns,
    per,
    own_ref,
    model_hbm,
    observed_ref,
    weights_ref,
    mask_ref,
    first_ref,
    second_ref,
    out_ref,
    model_ref,
    lead_in,
    trail_in,
    lead_out,
    trail_out,
    pair_in,
    chip_sum,
    chip_in,
    column_in,
    lead_gain,
    trail_gain,
    lead_term,
    trail_term,
    sky,
    outer,
    residual,
    model_sem,
    own_send,
    own_recv,
    relay_send,
    relay_recv,
    back_send,
    back_recv,
):
    steps, padded, flat = own_ref.shape
    channels, times, _, dirs, lanes = model_hbm.shape
    tiles = dirs // 8
    me = lax.axis_index("bl")
    row = me // GROUP
    place = lax.rem(me, GROUP)
    chip = place // 2
    core = lax.rem(place, 2)
    sibling = me + 1 - 2 * core

    def chip_peer(offset):
        return row * GROUP + lax.rem(chip + offset, CHIPS) * 2 + core

    def column_peer(offset):
        return lax.rem(row + offset, columns) * GROUP + place

    peers = [sibling]
    peers += [chip_peer(offset) for offset in range(1, CHIPS)]
    peers += [column_peer(offset) for offset in range(1, columns)]

    def remote(source, target, send, recv, device):
        return pltpu.make_async_remote_copy(
            src_ref=source,
            dst_ref=target,
            send_sem=send,
            recv_sem=recv,
            device_id={"bl": device},
            device_id_type=pl.DeviceIdType.MESH,
        )

    def model_copy(step):
        part = pl.ds(step * PAIR, PAIR)
        return pltpu.make_async_copy(model_hbm.at[part], model_ref.at[part], model_sem.at[step])

    def own_copies(step):
        copies = []
        for at, peer in enumerate(peers):
            if at < CHIPS:
                target = lead_in.at[step, place]
            else:
                target = trail_in.at[step, row]
            copies.append(
                remote(own_ref.at[step], target, own_send.at[step, at], own_recv.at[step, at], peer)
            )
        return copies

    def relay_copies(step):
        copies = []
        for offset in range(1, CHIPS):
            source = lax.rem(chip + CHIPS - offset, CHIPS) * 2 + core
            copies.append(
                remote(
                    lead_in.at[step, source],
                    lead_in.at[step, source],
                    relay_send.at[step, offset - 1],
                    relay_recv.at[step, offset - 1],
                    sibling,
                )
            )
        return copies

    def pair_copies(step):
        return [
            remote(
                lead_out.at[step, at * 2 + 1 - core],
                pair_in.at[step, at],
                back_send.at[step, at],
                back_recv.at[step, at],
                sibling,
            )
            for at in range(CHIPS)
        ]

    def column_copies(step):
        copies = []
        for offset in range(1, columns):
            sem_at = CHIPS + CHIPS - 1 + offset - 1
            copies.append(
                remote(
                    trail_out.at[step, lax.rem(row + offset, columns)],
                    column_in.at[step, offset - 1],
                    back_send.at[step, sem_at],
                    back_recv.at[step, sem_at],
                    column_peer(offset),
                )
            )
        return copies

    def chip_copies(step):
        copies = []
        for offset in range(1, CHIPS):
            sem_at = CHIPS + offset - 1
            copies.append(
                remote(
                    chip_sum.at[step, lax.rem(chip + offset, CHIPS)],
                    chip_in.at[step, offset - 1],
                    back_send.at[step, sem_at],
                    back_recv.at[step, sem_at],
                    chip_peer(offset),
                )
            )
        return copies

    def add_pair(step):
        for copy in pair_copies(step):
            copy.wait_recv()
        for at in range(CHIPS):
            chip_sum[step, at] = lead_out[step, at * 2 + core] + pair_in[step, at]
        for copy in chip_copies(step):
            copy.start()

    def channel(at, step):
        c = step * PAIR + at
        base = at * 8 * dirs

        def rows(q, tile):
            return pl.ds(pl.multiple_of(base + q * dirs + tile * 8, 8), 8)

        def stage(t, carry):
            block = model_ref[c, t].astype(F32)
            sky[t, 0:8] = block
            sky[t, 8:12] = block[0:4] + block[4:8]
            return carry

        lax.fori_loop(0, times, stage, 0)

        def outer_tile(tile, carry):
            lead = [lead_gain[rows(q, tile), :] for q in range(8)]
            trail = [trail_gain[rows(q, tile), :] for q in range(8)]
            for left in range(4):
                for right in range(4):
                    lr, li, tr, ti = lead[left], lead[4 + left], trail[right], trail[4 + right]
                    real = lr * tr + li * ti
                    imag = li * tr - lr * ti
                    slot = (left * 4 + right) * 3
                    outer[tile, slot] = real
                    outer[tile, slot + 1] = imag
                    outer[tile, slot + 2] = real + imag
            return carry

        lax.fori_loop(0, tiles, outer_tile, 0)

        def predict(pair_at, carry):
            sums = [[[None] * 3 for _ in range(4)] for _ in range(2)]
            for tile in range(tiles):
                part = pl.ds(tile * 8, 8)
                for k in range(2):
                    for l in range(2):
                        model = [
                            [sky[pair_at * 2 + u, 4 * z + 2 * k + l, part, :] for z in range(3)]
                            for u in range(2)
                        ]
                        for i in range(2):
                            for j in range(2):
                                slot = ((2 * i + k) * 4 + 2 * j + l) * 3
                                for z in range(3):
                                    gain = outer[tile, slot + z]
                                    for u in range(2):
                                        term = gain * model[u][z]
                                        old = sums[u][2 * i + j][z]
                                        sums[u][2 * i + j][z] = term if old is None else old + term
            for u in range(2):
                t = pair_at * 2 + u
                live = weights_ref[c, pl.ds(t, 1), :] * mask_ref[c, pl.ds(t, 1), :].astype(F32)
                for e in range(4):
                    one, two, three = sums[u][e]
                    real = jnp.sum(one - two, axis=0, keepdims=True)
                    imag = jnp.sum(three - one - two, axis=0, keepdims=True)
                    real = (observed_ref[c, t, e : e + 1, :] - real) * live
                    imag = (observed_ref[c, t, 4 + e : 5 + e, :] - imag) * live
                    residual[t, 3 * e] = jnp.broadcast_to(real, (8, lanes))
                    residual[t, 3 * e + 1] = jnp.broadcast_to(imag, (8, lanes))
                    residual[t, 3 * e + 2] = jnp.broadcast_to(imag - real, (8, lanes))
            return carry

        lax.fori_loop(0, times // 2, predict, 0)

        def gradient(tile, carry):
            part = pl.ds(pl.multiple_of(tile * 8, 8), 8)
            back = [None] * 8

            def add(total, term):
                return term if total is None else total + term

            for i in range(2):
                sums = [[[None] * 3 for _ in range(4)] for _ in range(2)]
                for t in range(times):
                    rest = [
                        [residual[t, 3 * (2 * i + j) + z] for z in range(3)] for j in range(2)
                    ]
                    for e in range(4):
                        for z in range(3):
                            model = sky[t, 4 * z + e, part, :]
                            for j in range(2):
                                sums[j][e][z] = add(sums[j][e][z], rest[j][z] * model)
                front = [None] * 4
                for j in range(2):
                    for e in range(4):
                        k, l = e // 2, e % 2
                        one, two, three = sums[j][e]
                        real = one + two
                        imag = three + (one - two)
                        tr = trail_gain[rows(2 * j + l, tile), :]
                        ti = trail_gain[rows(4 + 2 * j + l, tile), :]
                        lr = lead_gain[rows(2 * i + k, tile), :]
                        li = lead_gain[rows(4 + 2 * i + k, tile), :]
                        front[k] = add(front[k], real * tr - imag * ti)
                        front[2 + k] = add(front[2 + k], real * ti + imag * tr)
                        to = 2 * j + l
                        back[to] = add(back[to], real * lr + imag * li)
                        back[4 + to] = add(back[4 + to], real * li - imag * lr)
                for k in range(2):
                    lead_term[rows(2 * i + k, tile), :] = front[k]
                    lead_term[rows(4 + 2 * i + k, tile), :] = front[2 + k]
            for q in range(8):
                trail_term[rows(q, tile), :] = back[q]
            return carry

        lax.fori_loop(0, tiles, gradient, 0)
        return step

    barrier = pltpu.get_barrier_semaphore()
    for step in range(steps):
        model_copy(step).start()
    for peer in peers:
        pl.semaphore_signal(
            barrier, inc=1, device_id={"bl": peer}, device_id_type=pl.DeviceIdType.MESH
        )
    pl.semaphore_wait(barrier, len(peers))

    def begin(step, carry):
        for copy in own_copies(step):
            copy.start()
        lead_in[step, place] = own_ref[step]
        trail_in[step, row] = own_ref[step]
        return carry

    lax.fori_loop(0, steps, begin, 0)

    def hot(count, ids, leading):
        at = lax.broadcasted_iota(jnp.int32, (count * padded, lanes), 0)
        owner, inner = at // padded, at % padded
        owner = row * GROUP + owner if leading else owner * GROUP + place
        wanted = jnp.where(inner < per, owner * per + inner, -1)
        return jnp.where(wanted == ids, 1.0, 0.0).astype(BF16)

    lead_hot = hot(GROUP, first_ref[...], True)
    trail_hot = hot(columns, second_ref[...], False)
    inner = ((0,), (0,))
    outer_dims = ((1,), (1,))

    def work(step, carry):
        own = own_copies(step)
        relay = relay_copies(step)
        for offset in range(1, CHIPS):
            own[offset].wait_recv()
            relay[offset - 1].start()
        own[0].wait_recv()
        for copy in own[CHIPS:]:
            copy.wait_recv()
        block = trail_in[step].reshape(columns * padded, flat)
        trail_gain[...] = split_dot(block, trail_hot, inner, True)
        model_copy(step).wait()
        for copy in relay:
            copy.wait_recv()
        block = lead_in[step].reshape(GROUP * padded, flat)
        lead_gain[...] = split_dot(block, lead_hot, inner, True)
        lax.fori_loop(0, PAIR, channel, step)
        block = split_dot(lead_hot, lead_term[...], outer_dims, False)
        lead_out[step] = block.reshape(GROUP, padded, flat)
        for copy in pair_copies(step):
            copy.start()
        block = split_dot(trail_hot, trail_term[...], outer_dims, False)
        trail_out[step] = block.reshape(columns, padded, flat)
        for copy in column_copies(step):
            copy.start()
        add_pair(step)
        return carry

    lax.fori_loop(0, steps, work, 0)

    def finish(step, carry):
        total = chip_sum[step, chip] + trail_out[step, row]
        for at, copy in enumerate(column_copies(step)):
            copy.wait_recv()
            total = total + column_in[step, at]
        for at, copy in enumerate(chip_copies(step)):
            copy.wait_recv()
            total = total + chip_in[step, at]
        out_ref[step] = -total
        everything = own_copies(step) + relay_copies(step)
        everything += pair_copies(step) + chip_copies(step) + column_copies(step)
        for copy in everything:
            copy.wait_send()
        return carry

    lax.fori_loop(0, steps, finish, 0)


def body(
    station_gains,
    model_visibilities,
    observed,
    weights,
    kept_visibility_mask,
    first_station,
    second_station,
):
    columns = lax.axis_size("bl") // GROUP
    channels, comps, dirs, per = station_gains.shape
    times, lanes = weights.shape[1], weights.shape[2]
    steps = channels // PAIR
    flat = PAIR * comps * dirs
    padded = max(per, 8)
    own = jnp.transpose(station_gains.reshape(steps, flat, per), (0, 2, 1))
    own = jnp.pad(own, ((0, 0), (0, padded - per), (0, 0)))
    vmem = pl.BlockSpec(memory_space=pltpu.VMEM)
    chunk = (padded, flat)
    backs = CHIPS + CHIPS - 1 + columns - 1
    summed = pl.pallas_call(
        functools.partial(kernel, columns, per),
        out_shape=jax.ShapeDtypeStruct((steps,) + chunk, F32),
        in_specs=[vmem, pl.BlockSpec(memory_space=pl.ANY)] + [vmem] * 5,
        out_specs=vmem,
        scratch_shapes=[
            pltpu.VMEM(model_visibilities.shape, BF16),
            pltpu.VMEM((steps, GROUP) + chunk, F32),
            pltpu.VMEM((steps, columns) + chunk, F32),
            pltpu.VMEM((steps, GROUP) + chunk, F32),
            pltpu.VMEM((steps, columns) + chunk, F32),
            pltpu.VMEM((steps, CHIPS) + chunk, F32),
            pltpu.VMEM((steps, CHIPS) + chunk, F32),
            pltpu.VMEM((steps, CHIPS - 1) + chunk, F32),
            pltpu.VMEM((steps, columns - 1) + chunk, F32),
            pltpu.VMEM((flat, lanes), F32),
            pltpu.VMEM((flat, lanes), F32),
            pltpu.VMEM((flat, lanes), F32),
            pltpu.VMEM((flat, lanes), F32),
            pltpu.VMEM((times, 12, dirs, lanes), F32),
            pltpu.VMEM((dirs // 8, 48, 8, lanes), F32),
            pltpu.VMEM((times, 12, 8, lanes), F32),
            pltpu.SemaphoreType.DMA((steps,)),
            pltpu.SemaphoreType.DMA((steps, CHIPS + columns - 1)),
            pltpu.SemaphoreType.DMA((steps, CHIPS + columns - 1)),
            pltpu.SemaphoreType.DMA((steps, CHIPS - 1)),
            pltpu.SemaphoreType.DMA((steps, CHIPS - 1)),
            pltpu.SemaphoreType.DMA((steps, backs)),
            pltpu.SemaphoreType.DMA((steps, backs)),
        ],
        compiler_params=pltpu.CompilerParams(
            collective_id=0, has_side_effects=True, vmem_limit_bytes=48 * 1024 * 1024
        ),
    )(
        own,
        model_visibilities,
        observed,
        weights,
        kept_visibility_mask,
        first_station.reshape(1, lanes),
        second_station.reshape(1, lanes),
    )
    return jnp.transpose(summed[:, :per], (0, 2, 1)).reshape(station_gains.shape)


def solution(mesh):
    return jax.shard_map(
        body,
        mesh=mesh,
        in_specs=(
            P("grp", None, None, "bl"),
            P("grp", None, None, None, "bl"),
            P("grp", None, None, "bl"),
            P("grp", None, "bl"),
            P("grp", None, "bl"),
            P("bl"),
            P("bl"),
        ),
        out_specs=P("grp", None, None, "bl"),
        check_vma=False,
    )
```

```python
import functools

import jax
import jax.numpy as jnp
from jax import lax
from jax.experimental import pallas as pl
from jax.experimental.pallas import tpu as pltpu
from jax.sharding import PartitionSpec as P

GROUP = 8
CHIPS = GROUP // 2
PAIR = 2
F32 = jnp.float32
BF16 = jnp.bfloat16


def split_dot(lhs, rhs, dims, split_left):
    wide = lhs if split_left else rhs
    high = wide.astype(BF16)
    low = (wide - high.astype(F32)).astype(BF16)
    total = None
    for half in (high, low):
        pair = (half, rhs) if split_left else (lhs, half)
        term = lax.dot_general(*pair, (dims, ((), ())), preferred_element_type=F32)
        total = term if total is None else total + term
    return total


def kernel(
    columns,
    per,
    gains_hbm,
    model_hbm,
    observed_hbm,
    weights_hbm,
    mask_hbm,
    first_hbm,
    second_hbm,
    out_ref,
    gains_ref,
    model_ref,
    observed_ref,
    weights_ref,
    mask_ref,
    first_ref,
    second_ref,
    own_ref,
    lead_in,
    trail_in,
    lead_out,
    trail_out,
    pair_in,
    chip_sum,
    y_in,
    z_out,
    z_in,
    column_in,
    lead_gain,
    trail_gain,
    lead_term,
    trail_term,
    sky,
    outer,
    residual,
    gains_sem,
    model_sem,
    small_sem,
    go_send,
    go_recv,
    back_send,
    back_recv,
):
    steps, padded, flat = own_ref.shape
    channels, times, _, dirs, lanes = model_hbm.shape
    tiles = dirs // 8
    me = lax.axis_index("bl")
    row = me // GROUP
    place = lax.rem(me, GROUP)
    upper = place // 4
    lower = lax.rem(place // 2, 2)
    core = lax.rem(place, 2)

    def at_place(up, low, side):
        return up * 4 + low * 2 + side

    sib_place = at_place(upper, lower, 1 - core)
    y_place = at_place(upper, 1 - lower, core)
    z_place = at_place(1 - upper, lower, core)
    far_place = at_place(1 - upper, 1 - lower, core)
    base_device = row * GROUP
    sibling = base_device + sib_place
    y_peer = base_device + y_place
    z_peer = base_device + z_place

    def column_peer(offset):
        return lax.rem(row + offset, columns) * GROUP + place

    peers = [sibling, y_peer, z_peer]
    peers += [column_peer(offset) for offset in range(1, columns)]

    def remote(source, target, send, recv, device):
        return pltpu.make_async_remote_copy(
            src_ref=source,
            dst_ref=target,
            send_sem=send,
            recv_sem=recv,
            device_id={"bl": device},
            device_id_type=pl.DeviceIdType.MESH,
        )

    def model_copy(step):
        part = pl.ds(step * PAIR, PAIR)
        return pltpu.make_async_copy(model_hbm.at[part], model_ref.at[part], model_sem.at[step])

    def gains_copy(step):
        part = pl.ds(step * PAIR, PAIR)
        return pltpu.make_async_copy(gains_hbm.at[part], gains_ref.at[part], gains_sem.at[step])

    small = [
        pltpu.make_async_copy(source, target, small_sem.at[at])
        for at, (source, target) in enumerate(
            (
                (first_hbm, first_ref),
                (second_hbm, second_ref),
                (observed_hbm, observed_ref),
                (weights_hbm, weights_ref),
                (mask_hbm, mask_ref),
            )
        )
    ]

    def go(step, at, source, target, device):
        return remote(source, target, go_send.at[step, at], go_recv.at[step, at], device)

    def relay(step, at, slot, device):
        return go(step, at, lead_in.at[step, slot], lead_in.at[step, slot], device)

    def own_to(step, at, device):
        return go(step, at, own_ref.at[step], lead_in.at[step, place], device)

    def go_sib(step):
        return own_to(step, 0, sibling)

    def go_y(step):
        return own_to(step, 1, y_peer)

    def go_z(step):
        return own_to(step, 2, z_peer)

    def go_far(step):
        return relay(step, 3, z_place, y_peer)

    def pass_y(step):
        return relay(step, 4, y_place, sibling)

    def pass_z(step):
        return relay(step, 5, z_place, sibling)

    def pass_far(step):
        return relay(step, 6, far_place, sibling)

    def go_columns(step):
        return [
            go(step, 6 + offset, own_ref.at[step], trail_in.at[step, row], column_peer(offset))
            for offset in range(1, columns)
        ]

    def send_own(step):
        go_z(step).start()
        go_y(step).start()
        for copy in go_columns(step):
            copy.start()
        go_sib(step).start()

    def pass_near(step):
        go_z(step).wait_recv()
        go_far(step).start()
        pass_z(step).start()
        go_y(step).wait_recv()
        pass_y(step).start()

    def pass_last(step):
        go_far(step).wait_recv()
        pass_far(step).start()

    def back(step, at, source, target, device):
        return remote(source, target, back_send.at[step, at], back_recv.at[step, at], device)

    def pair_copies(step):
        return [
            back(
                step, at, lead_out.at[step, at * 2 + 1 - core], pair_in.at[step, at], sibling
            )
            for at in range(CHIPS)
        ]

    def y_copies(step):
        return [
            back(step, CHIPS, chip_sum.at[step, far_place // 2], y_in.at[step, 1], y_peer),
            back(step, CHIPS + 1, chip_sum.at[step, y_place // 2], y_in.at[step, 0], y_peer),
        ]

    def z_copy(step):
        return back(step, CHIPS + 2, z_out.at[step], z_in.at[step], z_peer)

    def column_copies(step):
        return [
            back(
                step,
                CHIPS + 2 + offset,
                trail_out.at[step, lax.rem(row + offset, columns)],
                column_in.at[step, offset - 1],
                column_peer(offset),
            )
            for offset in range(1, columns)
        ]

    def add_pair(step):
        for copy in pair_copies(step):
            copy.wait_recv()
        for at in range(CHIPS):
            chip_sum[step, at] = lead_out[step, at * 2 + core] + pair_in[step, at]
        for copy in y_copies(step):
            copy.start()

    def add_y(step):
        for copy in y_copies(step):
            copy.wait_recv()
        z_out[step] = chip_sum[step, z_place // 2] + y_in[step, 1]
        z_copy(step).start()

    def pack(step):
        gains_copy(step).wait()
        own = jnp.concatenate(
            [gains_ref[step * PAIR + at, q] for at in range(PAIR) for q in range(8)], axis=1
        )
        own_ref[step] = own
        lead_in[step, place] = own
        trail_in[step, row] = own

    def channel(at, step):
        c = step * PAIR + at
        base = at * 8 * dirs

        def rows(q, tile):
            return pl.ds(pl.multiple_of(base + q * dirs + tile * 8, 8), 8)

        def stage(t, carry):
            block = model_ref[c, t].astype(F32)
            sky[t, 0:8] = block
            sky[t, 8:12] = block[0:4] + block[4:8]
            return carry

        lax.fori_loop(0, times, stage, 0)

        def outer_tile(tile, carry):
            lead = [lead_gain[rows(q, tile), :] for q in range(8)]
            trail = [trail_gain[rows(q, tile), :] for q in range(8)]
            for left in range(4):
                for right in range(4):
                    lr, li, tr, ti = lead[left], lead[4 + left], trail[right], trail[4 + right]
                    real = lr * tr + li * ti
                    imag = li * tr - lr * ti
                    slot = (left * 4 + right) * 3
                    outer[tile, slot] = real
                    outer[tile, slot + 1] = imag
                    outer[tile, slot + 2] = real + imag
            return carry

        lax.fori_loop(0, tiles, outer_tile, 0)

        def predict(pair_at, carry):
            sums = [[[None] * 3 for _ in range(4)] for _ in range(2)]
            for tile in range(tiles):
                part = pl.ds(tile * 8, 8)
                for k in range(2):
                    for l in range(2):
                        model = [
                            [sky[pair_at * 2 + u, 4 * z + 2 * k + l, part, :] for z in range(3)]
                            for u in range(2)
                        ]
                        for i in range(2):
                            for j in range(2):
                                slot = ((2 * i + k) * 4 + 2 * j + l) * 3
                                for z in range(3):
                                    gain = outer[tile, slot + z]
                                    for u in range(2):
                                        term = gain * model[u][z]
                                        old = sums[u][2 * i + j][z]
                                        sums[u][2 * i + j][z] = term if old is None else old + term
            for u in range(2):
                t = pair_at * 2 + u
                live = weights_ref[c, pl.ds(t, 1), :] * mask_ref[c, pl.ds(t, 1), :].astype(F32)
                for e in range(4):
                    one, two, three = sums[u][e]
                    real = jnp.sum(one - two, axis=0, keepdims=True)
                    imag = jnp.sum(three - one - two, axis=0, keepdims=True)
                    real = (observed_ref[c, t, e : e + 1, :] - real) * live
                    imag = (observed_ref[c, t, 4 + e : 5 + e, :] - imag) * live
                    residual[t, 3 * e] = jnp.broadcast_to(real, (8, lanes))
                    residual[t, 3 * e + 1] = jnp.broadcast_to(imag, (8, lanes))
                    residual[t, 3 * e + 2] = jnp.broadcast_to(imag - real, (8, lanes))
            return carry

        lax.fori_loop(0, times // 2, predict, 0)

        def gradient(tile, carry):
            part = pl.ds(pl.multiple_of(tile * 8, 8), 8)
            back = [None] * 8

            def add(total, term):
                return term if total is None else total + term

            for i in range(2):
                sums = [[[None] * 3 for _ in range(4)] for _ in range(2)]
                for t in range(times):
                    rest = [
                        [residual[t, 3 * (2 * i + j) + z] for z in range(3)] for j in range(2)
                    ]
                    for e in range(4):
                        for z in range(3):
                            model = sky[t, 4 * z + e, part, :]
                            for j in range(2):
                                sums[j][e][z] = add(sums[j][e][z], rest[j][z] * model)
                front = [None] * 4
                for j in range(2):
                    for e in range(4):
                        k, l = e // 2, e % 2
                        one, two, three = sums[j][e]
                        real = one + two
                        imag = three + (one - two)
                        tr = trail_gain[rows(2 * j + l, tile), :]
                        ti = trail_gain[rows(4 + 2 * j + l, tile), :]
                        lr = lead_gain[rows(2 * i + k, tile), :]
                        li = lead_gain[rows(4 + 2 * i + k, tile), :]
                        front[k] = add(front[k], real * tr - imag * ti)
                        front[2 + k] = add(front[2 + k], real * ti + imag * tr)
                        to = 2 * j + l
                        back[to] = add(back[to], real * lr + imag * li)
                        back[4 + to] = add(back[4 + to], real * li - imag * lr)
                for k in range(2):
                    lead_term[rows(2 * i + k, tile), :] = front[k]
                    lead_term[rows(4 + 2 * i + k, tile), :] = front[2 + k]
            for q in range(8):
                trail_term[rows(q, tile), :] = back[q]
            return carry

        lax.fori_loop(0, tiles, gradient, 0)

    for step in range(steps):
        gains_copy(step).start()
    for copy in small:
        copy.start()
    for step in range(steps):
        model_copy(step).start()
    barrier = pltpu.get_barrier_semaphore()
    for peer in peers:
        pl.semaphore_signal(
            barrier, inc=1, device_id={"bl": peer}, device_id_type=pl.DeviceIdType.MESH
        )
    pack(0)
    pl.semaphore_wait(barrier, len(peers))
    send_own(0)
    for step in range(1, steps):
        pack(step)

    def hot(count, ids, leading):
        at = lax.broadcasted_iota(jnp.int32, (count * padded, lanes), 0)
        owner, inner = at // padded, at % padded
        owner = row * GROUP + owner if leading else owner * GROUP + place
        wanted = jnp.where(inner < per, owner * per + inner, -1)
        return jnp.where(wanted == ids, 1.0, 0.0).astype(BF16)

    for copy in small:
        copy.wait()
    lead_hot = hot(GROUP, first_ref[...], True)
    trail_hot = hot(columns, second_ref[...], False)
    inner = ((0,), (0,))
    outer_dims = ((1,), (1,))
    pass_near(0)
    if steps > 1:
        send_own(1)
    pass_last(0)

    def work(step, carry):
        for copy in go_columns(step):
            copy.wait_recv()
        block = trail_in[step].reshape(columns * padded, flat)
        trail_gain[...] = split_dot(block, trail_hot, inner, True)
        model_copy(step).wait()
        for copy in (go_sib(step), pass_y(step), pass_z(step), pass_far(step)):
            copy.wait_recv()
        block = lead_in[step].reshape(GROUP * padded, flat)
        lead_gain[...] = split_dot(block, lead_hot, inner, True)
        channel(0, step)

        @pl.when(step + 1 < steps)
        def _():
            pass_near(step + 1)

        @pl.when(step + 2 < steps)
        def _():
            send_own(step + 2)

        @pl.when(step >= 1)
        def _():
            add_pair(step - 1)

        channel(1, step)
        block = split_dot(lead_hot, lead_term[...], outer_dims, False)
        lead_out[step] = block.reshape(GROUP, padded, flat)
        for copy in pair_copies(step):
            copy.start()

        @pl.when(step + 1 < steps)
        def _():
            pass_last(step + 1)

        block = split_dot(trail_hot, trail_term[...], outer_dims, False)
        trail_out[step] = block.reshape(columns, padded, flat)
        for copy in column_copies(step):
            copy.start()

        @pl.when(step >= 1)
        def _():
            add_y(step - 1)

        return carry

    lax.fori_loop(0, steps, work, 0)
    add_pair(steps - 1)
    add_y(steps - 1)

    def finish(step, carry):
        total = chip_sum[step, place // 2] + trail_out[step, row]
        for at, copy in enumerate(column_copies(step)):
            copy.wait_recv()
            total = total + column_in[step, at]
        z_copy(step).wait_recv()
        total = -(total + y_in[step, 0] + z_in[step])
        for at in range(PAIR):
            for q in range(8):
                start = (at * 8 + q) * dirs
                out_ref[step * PAIR + at, q] = total[:, start : start + dirs]
        everything = [go_sib(step), go_y(step), go_z(step), go_far(step)]
        everything += [pass_y(step), pass_z(step), pass_far(step), z_copy(step)]
        everything += go_columns(step) + pair_copies(step) + y_copies(step) + column_copies(step)
        for copy in everything:
            copy.wait_send()
        return carry

    lax.fori_loop(0, steps, finish, 0)


def body(
    station_gains,
    model_visibilities,
    observed,
    weights,
    kept_visibility_mask,
    first_station,
    second_station,
):
    columns = lax.axis_size("bl") // GROUP
    channels, comps, dirs, per = station_gains.shape
    times, lanes = weights.shape[1], weights.shape[2]
    steps = channels // PAIR
    flat = PAIR * comps * dirs
    padded = max(per, 8)
    gains = jnp.transpose(station_gains, (0, 1, 3, 2))
    gains = jnp.pad(gains, ((0, 0), (0, 0), (0, padded - per), (0, 0)))
    chunk = (padded, flat)

    def buffer(*lead):
        return pltpu.VMEM(lead + chunk, F32)

    def sems(*dims):
        return pltpu.SemaphoreType.DMA(dims)

    summed = pl.pallas_call(
        functools.partial(kernel, columns, per),
        out_shape=jax.ShapeDtypeStruct(gains.shape, F32),
        in_specs=[pl.BlockSpec(memory_space=pl.ANY)] * 7,
        out_specs=pl.BlockSpec(memory_space=pltpu.VMEM),
        scratch_shapes=[
            pltpu.VMEM(gains.shape, F32),
            pltpu.VMEM(model_visibilities.shape, BF16),
            pltpu.VMEM(observed.shape, F32),
            pltpu.VMEM(weights.shape, F32),
            pltpu.VMEM(weights.shape, jnp.int32),
            pltpu.VMEM((1, lanes), jnp.int32),
            pltpu.VMEM((1, lanes), jnp.int32),
            buffer(steps),
            buffer(steps, GROUP),
            buffer(steps, columns),
            buffer(steps, GROUP),
            buffer(steps, columns),
            buffer(steps, CHIPS),
            buffer(steps, CHIPS),
            buffer(steps, 2),
            buffer(steps),
            buffer(steps),
            buffer(steps, columns - 1),
            pltpu.VMEM((flat, lanes), F32),
            pltpu.VMEM((flat, lanes), F32),
            pltpu.VMEM((flat, lanes), F32),
            pltpu.VMEM((flat, lanes), F32),
            pltpu.VMEM((times, 12, dirs, lanes), F32),
            pltpu.VMEM((dirs // 8, 48, 8, lanes), F32),
            pltpu.VMEM((times, 12, 8, lanes), F32),
            sems(steps),
            sems(steps),
            sems(5),
            sems(steps, 6 + columns),
            sems(steps, 6 + columns),
            sems(steps, CHIPS + 2 + columns),
            sems(steps, CHIPS + 2 + columns),
        ],
        compiler_params=pltpu.CompilerParams(
            collective_id=0, has_side_effects=True, vmem_limit_bytes=60 * 1024 * 1024
        ),
    )(
        gains,
        model_visibilities,
        observed,
        weights,
        kept_visibility_mask,
        first_station.reshape(1, lanes),
        second_station.reshape(1, lanes),
    )
    return jnp.transpose(summed[:, :, :per], (0, 1, 3, 2))


def solution(mesh):
    return jax.shard_map(
        body,
        mesh=mesh,
        in_specs=(
            P("grp", None, None, "bl"),
            P("grp", None, None, None, "bl"),
            P("grp", None, None, "bl"),
            P("grp", None, "bl"),
            P("grp", None, "bl"),
            P("bl"),
            P("bl"),
        ),
        out_specs=P("grp", None, None, "bl"),
        check_vma=False,
    )
```

```python
import functools

import jax
import jax.numpy as jnp
from jax import lax
from jax.experimental import pallas as pl
from jax.experimental.pallas import tpu as pltpu
from jax.sharding import PartitionSpec as P

GROUP = 8
CHIPS = GROUP // 2
PAIR = 2
F32 = jnp.float32
BF16 = jnp.bfloat16


def split_dot(lhs, rhs, dims, split_left):
    wide = lhs if split_left else rhs
    high = wide.astype(BF16)
    low = (wide - high.astype(F32)).astype(BF16)
    total = None
    for half in (high, low):
        pair = (half, rhs) if split_left else (lhs, half)
        term = lax.dot_general(*pair, (dims, ((), ())), preferred_element_type=F32)
        total = term if total is None else total + term
    return total


def kernel(
    columns,
    per,
    gains_hbm,
    model_hbm,
    observed_hbm,
    weights_hbm,
    mask_hbm,
    first_hbm,
    second_hbm,
    out_ref,
    gains_ref,
    model_ref,
    observed_ref,
    weights_ref,
    mask_ref,
    first_ref,
    second_ref,
    own_ref,
    lead_in,
    trail_in,
    lead_out,
    trail_out,
    pair_in,
    chip_sum,
    y_in,
    z_out,
    z_in,
    column_in,
    lead_gain,
    trail_gain,
    lead_term,
    trail_term,
    sky,
    outer,
    residual,
    gains_sem,
    model_sem,
    small_sem,
    go_send,
    go_recv,
    back_send,
    back_recv,
):
    steps, padded, flat = own_ref.shape
    assert steps == 4
    channels, times, _, dirs, lanes = model_hbm.shape
    tiles = dirs // 8
    me = lax.axis_index("bl")
    row = me // GROUP
    place = lax.rem(me, GROUP)
    upper = place // 4
    lower = lax.rem(place // 2, 2)
    core = lax.rem(place, 2)

    def at_place(up, low, side):
        return up * 4 + low * 2 + side

    sib_place = at_place(upper, lower, 1 - core)
    y_place = at_place(upper, 1 - lower, core)
    z_place = at_place(1 - upper, lower, core)
    far_place = at_place(1 - upper, 1 - lower, core)
    base_device = row * GROUP
    sibling = base_device + sib_place
    y_peer = base_device + y_place
    z_peer = base_device + z_place

    def column_peer(offset):
        return lax.rem(row + offset, columns) * GROUP + place

    peers = [sibling, y_peer, z_peer, base_device + far_place]
    peers += [column_peer(offset) for offset in range(1, columns)]

    def remote(source, target, send, recv, device):
        return pltpu.make_async_remote_copy(
            src_ref=source,
            dst_ref=target,
            send_sem=send,
            recv_sem=recv,
            device_id={"bl": device},
            device_id_type=pl.DeviceIdType.MESH,
        )

    def model_copy(step):
        part = pl.ds(step * PAIR, PAIR)
        return pltpu.make_async_copy(model_hbm.at[part], model_ref.at[part], model_sem.at[step])

    def gains_copy(step):
        part = pl.ds(step * PAIR, PAIR)
        return pltpu.make_async_copy(gains_hbm.at[part], gains_ref.at[part], gains_sem.at[step])

    small = [
        pltpu.make_async_copy(source, target, small_sem.at[at])
        for at, (source, target) in enumerate(
            (
                (first_hbm, first_ref),
                (second_hbm, second_ref),
                (observed_hbm, observed_ref),
                (weights_hbm, weights_ref),
                (mask_hbm, mask_ref),
            )
        )
    ]

    def go(step, at, source, target, device):
        return remote(source, target, go_send.at[step, at], go_recv.at[step, at], device)

    def relay(step, at, slot, device):
        return go(step, at, lead_in.at[step, slot], lead_in.at[step, slot], device)

    def own_to(step, at, device):
        return go(step, at, own_ref.at[step], lead_in.at[step, place], device)

    def go_sib(step):
        return own_to(step, 0, sibling)

    def go_y(step):
        return own_to(step, 1, y_peer)

    def go_z(step):
        return own_to(step, 2, z_peer)

    def go_far(step):
        return own_to(step, 3, base_device + far_place)

    def pass_y(step):
        return relay(step, 4, y_place, sibling)

    def pass_z(step):
        return relay(step, 5, z_place, sibling)

    def pass_far(step):
        return relay(step, 6, far_place, sibling)

    def go_columns(step):
        return [
            go(step, 6 + offset, own_ref.at[step], trail_in.at[step, row], column_peer(offset))
            for offset in range(1, columns)
        ]

    def send_own(step):
        go_z(step).start()
        go_y(step).start()
        go_far(step).start()
        for copy in go_columns(step):
            copy.start()
        go_sib(step).start()

    def pass_near(step):
        go_z(step).wait_recv()
        pass_z(step).start()
        go_y(step).wait_recv()
        pass_y(step).start()

    def pass_last(step):
        go_far(step).wait_recv()
        pass_far(step).start()

    def back(step, at, source, target, device):
        return remote(source, target, back_send.at[step, at], back_recv.at[step, at], device)

    def pair_copies(step):
        return [
            back(
                step, at, lead_out.at[step, at * 2 + 1 - core], pair_in.at[step, at], sibling
            )
            for at in range(CHIPS)
        ]

    def y_copies(step):
        return [
            back(step, CHIPS, chip_sum.at[step, far_place // 2], y_in.at[step, 1], y_peer),
            back(step, CHIPS + 1, chip_sum.at[step, y_place // 2], y_in.at[step, 0], y_peer),
        ]

    def z_copy(step):
        return back(step, CHIPS + 2, z_out.at[step], z_in.at[step], z_peer)

    def column_copies(step):
        return [
            back(
                step,
                CHIPS + 2 + offset,
                trail_out.at[step, lax.rem(row + offset, columns)],
                column_in.at[step, offset - 1],
                column_peer(offset),
            )
            for offset in range(1, columns)
        ]

    def add_pair(step):
        for copy in pair_copies(step):
            copy.wait_recv()
        for at in range(CHIPS):
            chip_sum[step, at] = lead_out[step, at * 2 + core] + pair_in[step, at]
        for copy in y_copies(step):
            copy.start()

    def add_y(step):
        for copy in y_copies(step):
            copy.wait_recv()
        z_out[step] = chip_sum[step, z_place // 2] + y_in[step, 1]
        z_copy(step).start()

    def pack(step):
        gains_copy(step).wait()
        own = jnp.concatenate(
            [gains_ref[step * PAIR + at, q] for at in range(PAIR) for q in range(8)], axis=1
        )
        own_ref[step] = own
        lead_in[step, place] = own
        trail_in[step, row] = own

    def channel(at, step):
        c = step * PAIR + at
        base = at * 8 * dirs

        def rows(q, tile):
            return pl.ds(pl.multiple_of(base + q * dirs + tile * 8, 8), 8)

        def stage(t, carry):
            block = model_ref[c, t].astype(F32)
            sky[t, 0:8] = block
            sky[t, 8:12] = block[0:4] + block[4:8]
            return carry

        lax.fori_loop(0, times, stage, 0)

        def outer_tile(tile, carry):
            lead = [lead_gain[rows(q, tile), :] for q in range(8)]
            trail = [trail_gain[rows(q, tile), :] for q in range(8)]
            for left in range(4):
                for right in range(4):
                    lr, li, tr, ti = lead[left], lead[4 + left], trail[right], trail[4 + right]
                    real = lr * tr + li * ti
                    imag = li * tr - lr * ti
                    slot = (left * 4 + right) * 3
                    outer[tile, slot] = real
                    outer[tile, slot + 1] = imag
                    outer[tile, slot + 2] = real + imag
            return carry

        lax.fori_loop(0, tiles, outer_tile, 0)

        def predict(pair_at, carry):
            sums = [[[None] * 3 for _ in range(4)] for _ in range(2)]
            for tile in range(tiles):
                part = pl.ds(tile * 8, 8)
                for k in range(2):
                    for l in range(2):
                        model = [
                            [sky[pair_at * 2 + u, 4 * z + 2 * k + l, part, :] for z in range(3)]
                            for u in range(2)
                        ]
                        for i in range(2):
                            for j in range(2):
                                slot = ((2 * i + k) * 4 + 2 * j + l) * 3
                                for z in range(3):
                                    gain = outer[tile, slot + z]
                                    for u in range(2):
                                        term = gain * model[u][z]
                                        old = sums[u][2 * i + j][z]
                                        sums[u][2 * i + j][z] = term if old is None else old + term
            for u in range(2):
                t = pair_at * 2 + u
                live = weights_ref[c, pl.ds(t, 1), :] * mask_ref[c, pl.ds(t, 1), :].astype(F32)
                for e in range(4):
                    one, two, three = sums[u][e]
                    real = jnp.sum(one - two, axis=0, keepdims=True)
                    imag = jnp.sum(three - one - two, axis=0, keepdims=True)
                    real = (observed_ref[c, t, e : e + 1, :] - real) * live
                    imag = (observed_ref[c, t, 4 + e : 5 + e, :] - imag) * live
                    residual[t, 3 * e] = jnp.broadcast_to(real, (8, lanes))
                    residual[t, 3 * e + 1] = jnp.broadcast_to(imag, (8, lanes))
                    residual[t, 3 * e + 2] = jnp.broadcast_to(imag - real, (8, lanes))
            return carry

        lax.fori_loop(0, times // 2, predict, 0)

        def gradient(tile, carry):
            part = pl.ds(pl.multiple_of(tile * 8, 8), 8)
            back = [None] * 8

            def add(total, term):
                return term if total is None else total + term

            for i in range(2):
                sums = [[[None] * 3 for _ in range(4)] for _ in range(2)]
                for t in range(times):
                    rest = [
                        [residual[t, 3 * (2 * i + j) + z] for z in range(3)] for j in range(2)
                    ]
                    for e in range(4):
                        for z in range(3):
                            model = sky[t, 4 * z + e, part, :]
                            for j in range(2):
                                sums[j][e][z] = add(sums[j][e][z], rest[j][z] * model)
                front = [None] * 4
                for j in range(2):
                    for e in range(4):
                        k, l = e // 2, e % 2
                        one, two, three = sums[j][e]
                        real = one + two
                        imag = three + (one - two)
                        tr = trail_gain[rows(2 * j + l, tile), :]
                        ti = trail_gain[rows(4 + 2 * j + l, tile), :]
                        lr = lead_gain[rows(2 * i + k, tile), :]
                        li = lead_gain[rows(4 + 2 * i + k, tile), :]
                        front[k] = add(front[k], real * tr - imag * ti)
                        front[2 + k] = add(front[2 + k], real * ti + imag * tr)
                        to = 2 * j + l
                        back[to] = add(back[to], real * lr + imag * li)
                        back[4 + to] = add(back[4 + to], real * li - imag * lr)
                for k in range(2):
                    lead_term[rows(2 * i + k, tile), :] = front[k]
                    lead_term[rows(4 + 2 * i + k, tile), :] = front[2 + k]
            for q in range(8):
                trail_term[rows(q, tile), :] = back[q]
            return carry

        lax.fori_loop(0, tiles, gradient, 0)

    for step in range(steps):
        gains_copy(step).start()
    for copy in small:
        copy.start()
    for step in range(steps):
        model_copy(step).start()
    barrier = pltpu.get_barrier_semaphore()
    for peer in peers:
        pl.semaphore_signal(
            barrier, inc=1, device_id={"bl": peer}, device_id_type=pl.DeviceIdType.MESH
        )
    pack(0)
    pl.semaphore_wait(barrier, len(peers))
    send_own(0)
    for step in range(1, steps):
        pack(step)

    def hot(count, ids, leading):
        at = lax.broadcasted_iota(jnp.int32, (count * padded, lanes), 0)
        owner, inner = at // padded, at % padded
        owner = row * GROUP + owner if leading else owner * GROUP + place
        wanted = jnp.where(inner < per, owner * per + inner, -1)
        return jnp.where(wanted == ids, 1.0, 0.0).astype(BF16)

    for copy in small:
        copy.wait()
    lead_hot = hot(GROUP, first_ref[...], True)
    trail_hot = hot(columns, second_ref[...], False)
    inner = ((0,), (0,))
    outer_dims = ((1,), (1,))
    pass_near(0)
    send_own(1)
    pass_last(0)

    def work(step, carry):
        for copy in go_columns(step):
            copy.wait_recv()
        block = trail_in[step].reshape(columns * padded, flat)
        trail_gain[...] = split_dot(block, trail_hot, inner, True)
        model_copy(step).wait()
        for copy in (go_sib(step), pass_y(step), pass_z(step), pass_far(step)):
            copy.wait_recv()
        block = lead_in[step].reshape(GROUP * padded, flat)
        lead_gain[...] = split_dot(block, lead_hot, inner, True)

        @pl.when(step >= 1)
        def _():
            add_pair(step - 1)

        channel(0, step)

        @pl.when(step == 0)
        def _():
            pass_near(1)
            send_own(2)

        @pl.when(step == 1)
        def _():
            pass_near(2)

        channel(1, step)
        block = split_dot(lead_hot, lead_term[...], outer_dims, False)
        lead_out[step] = block.reshape(GROUP, padded, flat)
        for copy in pair_copies(step):
            copy.start()

        @pl.when(step == 0)
        def _():
            send_own(3)

        block = split_dot(trail_hot, trail_term[...], outer_dims, False)
        trail_out[step] = block.reshape(columns, padded, flat)
        for copy in column_copies(step):
            copy.start()

        @pl.when(step + 1 < steps)
        def _():
            pass_last(step + 1)

        @pl.when(step == 1)
        def _():
            pass_near(3)

        @pl.when(step >= 1)
        def _():
            add_y(step - 1)

        return carry

    lax.fori_loop(0, steps, work, 0)
    add_pair(steps - 1)
    add_y(steps - 1)

    def finish(step, carry):
        total = chip_sum[step, place // 2] + trail_out[step, row]
        for at, copy in enumerate(column_copies(step)):
            copy.wait_recv()
            total = total + column_in[step, at]
        z_copy(step).wait_recv()
        total = -(total + y_in[step, 0] + z_in[step])
        for at in range(PAIR):
            for q in range(8):
                start = (at * 8 + q) * dirs
                out_ref[step * PAIR + at, q] = total[:, start : start + dirs]
        everything = [go_sib(step), go_y(step), go_z(step), go_far(step)]
        everything += [pass_y(step), pass_z(step), pass_far(step), z_copy(step)]
        everything += go_columns(step) + pair_copies(step) + y_copies(step) + column_copies(step)
        for copy in everything:
            copy.wait_send()
        return carry

    lax.fori_loop(0, steps, finish, 0)


def body(
    station_gains,
    model_visibilities,
    observed,
    weights,
    kept_visibility_mask,
    first_station,
    second_station,
):
    columns = lax.axis_size("bl") // GROUP
    channels, comps, dirs, per = station_gains.shape
    times, lanes = weights.shape[1], weights.shape[2]
    steps = channels // PAIR
    flat = PAIR * comps * dirs
    padded = max(per, 8)
    gains = jnp.transpose(station_gains, (0, 1, 3, 2))
    gains = jnp.pad(gains, ((0, 0), (0, 0), (0, padded - per), (0, 0)))
    chunk = (padded, flat)

    def buffer(*lead):
        return pltpu.VMEM(lead + chunk, F32)

    def sems(*dims):
        return pltpu.SemaphoreType.DMA(dims)

    summed = pl.pallas_call(
        functools.partial(kernel, columns, per),
        out_shape=jax.ShapeDtypeStruct(gains.shape, F32),
        in_specs=[pl.BlockSpec(memory_space=pl.ANY)] * 7,
        out_specs=pl.BlockSpec(memory_space=pltpu.VMEM),
        scratch_shapes=[
            pltpu.VMEM(gains.shape, F32),
            pltpu.VMEM(model_visibilities.shape, BF16),
            pltpu.VMEM(observed.shape, F32),
            pltpu.VMEM(weights.shape, F32),
            pltpu.VMEM(weights.shape, jnp.int32),
            pltpu.VMEM((1, lanes), jnp.int32),
            pltpu.VMEM((1, lanes), jnp.int32),
            buffer(steps),
            buffer(steps, GROUP),
            buffer(steps, columns),
            buffer(steps, GROUP),
            buffer(steps, columns),
            buffer(steps, CHIPS),
            buffer(steps, CHIPS),
            buffer(steps, 2),
            buffer(steps),
            buffer(steps),
            buffer(steps, columns - 1),
            pltpu.VMEM((flat, lanes), F32),
            pltpu.VMEM((flat, lanes), F32),
            pltpu.VMEM((flat, lanes), F32),
            pltpu.VMEM((flat, lanes), F32),
            pltpu.VMEM((times, 12, dirs, lanes), F32),
            pltpu.VMEM((dirs // 8, 48, 8, lanes), F32),
            pltpu.VMEM((times, 12, 8, lanes), F32),
            sems(steps),
            sems(steps),
            sems(5),
            sems(steps, 6 + columns),
            sems(steps, 6 + columns),
            sems(steps, CHIPS + 2 + columns),
            sems(steps, CHIPS + 2 + columns),
        ],
        compiler_params=pltpu.CompilerParams(
            collective_id=0, has_side_effects=True, vmem_limit_bytes=60 * 1024 * 1024
        ),
    )(
        gains,
        model_visibilities,
        observed,
        weights,
        kept_visibility_mask,
        first_station.reshape(1, lanes),
        second_station.reshape(1, lanes),
    )
    return jnp.transpose(summed[:, :, :per], (0, 1, 3, 2))


def solution(mesh):
    return jax.shard_map(
        body,
        mesh=mesh,
        in_specs=(
            P("grp", None, None, "bl"),
            P("grp", None, None, None, "bl"),
            P("grp", None, None, "bl"),
            P("grp", None, "bl"),
            P("grp", None, "bl"),
            P("bl"),
            P("bl"),
        ),
        out_specs=P("grp", None, None, "bl"),
        check_vma=False,
    )
```
